32 devices in a mesh: dp: 8 (over y, x, core), tensor: 4 (over z).
Axes of the slice: x: 2, y: 2, z: 4, core: 2. Of those that a mesh axis runs over, the one named last changes fastest.
Arguments:
- inputs: bfloat16 [16384, 1024], P(('dp', 'tensor')), may hold values from -6 to 6
- cotangent: bfloat16 [16384, 1024], P(('dp', 'tensor')), may hold values from -6 to 6
- seq_lens: int32 [8, 64], P('dp'), may hold values from 0 to 512, as said below
- gains: float32 [2, 1024], P(None, 'dp'), may hold values from 0.5 to 1.5
- w_qkv: float32 [3, 1024, 1024], P(None, 'dp', 'tensor'), may hold values from -0.1875 to 0.1875
- w_out: float32 [1024, 1024], P('tensor', 'dp'), may hold values from -1 to 1
- w_in: float32 [2, 1024, 2624], P(None, 'dp', 'tensor'), may hold values from -0.1875 to 0.1875
- w_down: float32 [2624, 1024], P('tensor', 'dp'), may hold values from -0.125 to 0.125
- moment_gains: float32 [2, 1024], P(None, 'dp'), may hold values from -64 to 64
- square_gains: float32 [2, 1024], P(None, 'dp'), may hold values from 116.98176 to 1871.7081
- moment_qkv: float32 [3, 1024, 1024], P(None, 'dp', 'tensor'), may hold values from -32 to 32
- square_qkv: float32 [3, 1024, 1024], P(None, 'dp', 'tensor'), may hold values from 29.24544 to 467.92703
- moment_out: float32 [1024, 1024], P('tensor', 'dp'), may hold values from -8 to 8
- square_out: float32 [1024, 1024], P('tensor', 'dp'), may hold values from 1.6845373 to 26.952597
- moment_in: float32 [2, 1024, 2624], P(None, 'dp', 'tensor'), may hold values from -28 to 28
- square_in: float32 [2, 1024, 2624], P(None, 'dp', 'tensor'), may hold values from 18.717081 to 299.4733
- moment_down: float32 [2624, 1024], P('tensor', 'dp'), may hold values from -48 to 48
- square_down: float32 [2624, 1024], P('tensor', 'dp'), may hold values from 49.13234 to 786.11743
Outputs:
- outputs: float32 [16384, 1024], P(('dp', 'tensor'))
- grad_inputs: float32 [16384, 1024], P(('dp', 'tensor'))
- new_moment_gains: float32 [2, 1024], P(None, 'dp')
- new_square_gains: float32 [2, 1024], P(None, 'dp')
- new_gains: float32 [2, 1024], P(None, 'dp')
- new_moment_qkv: float32 [3, 1024, 1024], P(None, 'dp', 'tensor')
- new_square_qkv: float32 [3, 1024, 1024], P(None, 'dp', 'tensor')
- new_qkv: float32 [3, 1024, 1024], P(None, 'dp', 'tensor')
- new_moment_out: float32 [1024, 1024], P('tensor', 'dp')
- new_square_out: float32 [1024, 1024], P('tensor', 'dp')
- new_out: float32 [1024, 1024], P('tensor', 'dp')
- new_moment_in: float32 [2, 1024, 2624], P(None, 'dp', 'tensor')
- new_square_in: float32 [2, 1024, 2624], P(None, 'dp', 'tensor')
- new_in: float32 [2, 1024, 2624], P(None, 'dp', 'tensor')
- new_moment_down: float32 [2624, 1024], P('tensor', 'dp')
- new_square_down: float32 [2624, 1024], P('tensor', 'dp')
- new_down: float32 [2624, 1024], P('tensor', 'dp')
The draws below stay inside these ranges and needn't reach their ends.
Inputs may be any that keep to these rules, and one draw needn't show every extreme that they name: `seq_lens`: row g lists the lengths of data group g's sequences in their order in the group; used slots come first and the rest are 0; slot 0 holds a sequence of exactly 512; a row sums to at most 2048 and to at least 512.
All inputs are finite; a program needn't handle non-finite values.
Results may differ from the reference program's by a relative error of at most 0.013.
The reference program's roundings to bfloat16 on the way count: a program that leaves them out, or rounds other values in their place, can miss the bound.
Values may be sent and summed in bfloat16 or wider, within the bound.
A program may use at most 128 MiB of HBM per device.

```python
import math
import jax
import jax.numpy as jnp
from jax import lax

D = 1024
HEADS = 16
FF = 2624
MAXLEN = 512
QBLOCK = 512
STEP = 10
HEAD_DIM = 64
GROUP_TOK = 2048
GROUPS = 8
TOKENS = 16384
SLOTS = 64


def draw_seq_lens(key, part):
    key = jax.random.fold_in(key, 7)
    length_key, order_key = jax.random.split(key)
    shortest = max(1, MAXLEN // 16)
    lengths = jax.random.randint(length_key, (GROUPS, SLOTS), shortest, MAXLEN + 1, dtype=jnp.int32)
    lengths = lengths.at[:, 0].set(MAXLEN)
    ranks = jax.random.permutation(order_key, GROUPS).astype(jnp.int32)
    targets = GROUP_TOK * (35 + 65 * ranks // max(GROUPS - 1, 1)) // 100
    targets = jnp.maximum(targets, MAXLEN)
    ends = jnp.cumsum(lengths, axis=1)
    return jnp.where(ends <= targets[:, None], lengths, 0).astype(jnp.int32)


def levels(own_key, shape, shards, smallest, largest):
    loudness, own = 1.0, jax.random.fold_in(own_key, 6)
    for dim, blocks in shards:
        steps = jnp.exp(jax.random.uniform(jax.random.fold_in(own, dim), (blocks,), jnp.float32, smallest / len(shards), largest / len(shards)))
        loudness = loudness * jnp.repeat(steps, shape[dim] // blocks).reshape([-1 if axis == dim else 1 for axis in range(len(shape))])
    return loudness


def bell_draw(rng, shape, deviation, bound, cuts=(), held_as=jnp.bfloat16):
    entries = jax.random.normal(rng, shape, jnp.float32) * deviation
    if len(cuts) > 0:
        entries = levels(rng, shape, cuts, -0.22, 0.18) * entries
    return jnp.clip(entries, min=-bound, max=bound).astype(held_as)


def setup_inputs(seed: int = 0) -> dict:
    key_of = jax.random.split(jax.random.key(seed), 19)
    inputs = bell_draw(key_of[0], (TOKENS, D), 1.0, 6.0, ((0, 32),))
    cotangent = bell_draw(key_of[1], (TOKENS, D), 1.0, 6.0, ((0, 32),))
    seq_lens = draw_seq_lens(jax.random.fold_in(key_of[18], 71), 0)
    gains = jnp.clip(1.0 + 0.1 * jax.random.normal(key_of[3], (2, D), jnp.float32), 0.5, 1.5)
    w_qkv = bell_draw(key_of[4], (3, D, D), D ** -0.5, 0.1875, ((1, 8), (2, 4)), jnp.float32)
    w_out = bell_draw(key_of[5], (D, D), (D // 32) ** -0.5, 1.0, ((0, 4), (1, 8)), jnp.float32)
    w_in = bell_draw(key_of[6], (2, D, FF), D ** -0.5, 0.1875, ((1, 8), (2, 4)), jnp.float32)
    w_down = bell_draw(key_of[7], (FF, D), FF ** -0.5, 0.125, ((0, 4), (1, 8)), jnp.float32)
    moment_gains = bell_draw(key_of[8], (2, D), (0.11 * (0.7 * TOKENS) ** 0.5), 64.0, ((1, 8),), jnp.float32)
    square_gains = jnp.clip(jnp.exp(math.log(1871.7081) - 2.7725887 * jax.random.uniform(key_of[9], (2, D), jnp.float32) ** levels(key_of[9], (2, D), ((1, 8),), -0.2, 0.2)), 116.98176, 1871.7081)
    moment_qkv = bell_draw(key_of[10], (3, D, D), (0.11 * 0.5 * (0.7 * TOKENS) ** 0.5), 32.0, ((1, 8), (2, 4)), jnp.float32)
    square_qkv = jnp.clip(jnp.exp(math.log(467.92703) - 2.7725887 * jax.random.uniform(key_of[11], (3, D, D), jnp.float32) ** levels(key_of[11], (3, D, D), ((1, 8), (2, 4)), -0.2, 0.2)), 29.24544, 467.92703)
    moment_out = bell_draw(key_of[12], (D, D), (0.11 * 0.12 * (0.7 * TOKENS) ** 0.5), 8.0, ((0, 4), (1, 8)), jnp.float32)
    square_out = jnp.clip(jnp.exp(math.log(26.952597) - 2.7725887 * jax.random.uniform(key_of[13], (D, D), jnp.float32) ** levels(key_of[13], (D, D), ((0, 4), (1, 8)), -0.2, 0.2)), 1.6845373, 26.952597)
    moment_in = bell_draw(key_of[14], (2, D, FF), (0.11 * 0.4 * (0.7 * TOKENS) ** 0.5), 28.0, ((1, 8), (2, 4)), jnp.float32)
    square_in = jnp.clip(jnp.exp(math.log(299.4733) - 2.7725887 * jax.random.uniform(key_of[15], (2, D, FF), jnp.float32) ** levels(key_of[15], (2, D, FF), ((1, 8), (2, 4)), -0.2, 0.2)), 18.717081, 299.4733)
    moment_down = bell_draw(key_of[16], (FF, D), (0.11 * 0.65 * (0.7 * TOKENS) ** 0.5), 48.0, ((0, 4), (1, 8)), jnp.float32)
    square_down = jnp.clip(jnp.exp(math.log(786.11743) - 2.7725887 * jax.random.uniform(key_of[17], (FF, D), jnp.float32) ** levels(key_of[17], (FF, D), ((0, 4), (1, 8)), -0.2, 0.2)), 49.13234, 786.11743)
    return {"inputs": inputs, "cotangent": cotangent, "seq_lens": seq_lens, "gains": gains, "w_qkv": w_qkv, "w_out": w_out, "w_in": w_in, "w_down": w_down, "moment_gains": moment_gains, "square_gains": square_gains, "moment_qkv": moment_qkv, "square_qkv": square_qkv, "moment_out": moment_out, "square_out": square_out, "moment_in": moment_in, "square_in": square_in, "moment_down": moment_down, "square_down": square_down}


NORM_EPS = 1e-05
ROPE_BASE = 160000.0
NEG_LARGE = -1000000000.0
BETA_ONE = 0.9
BETA_TWO = 0.98
ADAM_EPS = 1e-06
LEARN_RATE = 0.05
GAIN_RATE = 0.2
WEIGHT_DECAY = 0.01
HIGHEST = lax.Precision.HIGHEST

@jax.custom_vjp
def low(v):
    return lax.optimization_barrier(v.astype(jnp.bfloat16)).astype(jnp.float32)

@jax.custom_vjp
def low_back(v):
    return v

def low_keep(v):
    return (low(v), None)

def low_pass(kept, grad):
    return (grad,)

def back_keep(v):
    return (v, None)

def back_low(kept, grad):
    return (low(grad),)
low.defvjp(low_keep, low_pass)
low_back.defvjp(back_keep, back_low)

def layout(lengths, count):
    ends = jnp.cumsum(lengths).astype(jnp.int32)
    starts = (ends - lengths).astype(jnp.int32)
    row_ids = jnp.arange(count, dtype=jnp.int32)
    member = (row_ids[:, None] >= starts[None, :]) & (row_ids[:, None] < ends[None, :])
    slot_ids = jnp.arange(lengths.shape[0], dtype=jnp.int32)
    valid = jnp.any(member, axis=1)
    segment = jnp.where(valid, lax.optimization_barrier(jnp.sum(jnp.where(member, slot_ids[None, :], 0), axis=1)), -1).astype(jnp.int32)
    position = (row_ids - lax.optimization_barrier(jnp.sum(jnp.where(member, starts[None, :], 0), axis=1))).astype(jnp.int32)
    return (segment, position, valid)

def rotary(values, position):
    head_size = values.shape[-1]
    half_size = head_size // 2
    exponents = jnp.arange(half_size, dtype=jnp.float32) * (2.0 / head_size)
    frequency = ROPE_BASE ** (-exponents)
    angles = position.astype(jnp.float32)[:, None] * frequency[None, :]
    cosine_table = jnp.concatenate([jnp.cos(angles), jnp.cos(angles)], axis=-1)[:, None, :]
    sine_table = jnp.concatenate([jnp.sin(angles), jnp.sin(angles)], axis=-1)[:, None, :]
    rotated = jnp.concatenate([-values[..., half_size:], values[..., :half_size]], axis=-1)
    return values * cosine_table + rotated * sine_table

def normalize(values):
    centered = values - lax.optimization_barrier(jnp.mean(values, axis=-1, keepdims=True))
    inverse = lax.rsqrt(lax.optimization_barrier(jnp.mean(centered * centered, axis=-1, keepdims=True)) + NORM_EPS)
    return (centered * inverse, inverse)

def allowed_mask(query_segment, query_index, key_segment, key_index):
    same = (query_segment[:, None] == key_segment[None, :]) & (query_segment[:, None] >= 0)
    return same | (query_index[:, None] == key_index[None, :])

def attention(queries, keys, values, segment):
    total = queries.shape[0]
    key_index = jnp.arange(total, dtype=jnp.int32)
    scale = HEAD_DIM ** (-0.5)

    def one_block(number):
        start = number * QBLOCK
        query_block = lax.dynamic_slice_in_dim(queries, start, QBLOCK, 0)
        query_segment = lax.dynamic_slice_in_dim(segment, start, QBLOCK, 0)
        query_index = start + jnp.arange(QBLOCK, dtype=jnp.int32)
        scores = low_back(jnp.einsum('qhd,khd->hqk', query_block, keys, precision=HIGHEST) * scale)
        allowed = allowed_mask(query_segment, query_index, segment, key_index)
        weights = low(jax.nn.softmax(jnp.where(allowed[None], scores, NEG_LARGE), axis=-1))
        return jnp.einsum('hqk,khd->qhd', weights, values, precision=HIGHEST)
    blocks = lax.map(jax.checkpoint(one_block), jnp.arange(total // QBLOCK, dtype=jnp.int32))
    return blocks.reshape(total, HEADS * HEAD_DIM)

def forward_group(residual, gains, w_qkv, w_out, w_in, w_down, segment, position):
    total = residual.shape[0]
    gains = low(gains)
    w_qkv = low(w_qkv)
    w_out = low(w_out)
    w_in = low(w_in)
    w_down = low(w_down)
    normed_one, unused = normalize(residual)
    first_rows = low(normed_one * gains[0])
    projected = low_back(jnp.einsum('rd,kdc->krc', first_rows, w_qkv, precision=HIGHEST))
    queries = low(rotary(projected[0].reshape(total, HEADS, HEAD_DIM), position))
    keys = low(rotary(projected[1].reshape(total, HEADS, HEAD_DIM), position))
    values = low(projected[2].reshape(total, HEADS, HEAD_DIM))
    attended = low(low_back(attention(queries, keys, values, segment)))
    middle = residual + low_back(jnp.dot(attended, w_out, precision=HIGHEST))
    normed_two, unused = normalize(middle)
    second_rows = low(normed_two * gains[1])
    expanded = low_back(jnp.einsum('rd,kdf->krf', second_rows, w_in, precision=HIGHEST))
    hidden = low(jax.nn.gelu(expanded[0], approximate=False) * expanded[1])
    return middle + low_back(jnp.dot(hidden, w_down, precision=HIGHEST))

def adam_step(param, grad, moment, square, rate, decay):
    moment = BETA_ONE * moment + (1.0 - BETA_ONE) * grad
    square = BETA_TWO * square + (1.0 - BETA_TWO) * grad * grad
    moment_hat = moment / (1.0 - BETA_ONE ** STEP)
    square_hat = square / (1.0 - BETA_TWO ** STEP)
    updated = param - rate * (moment_hat / (jnp.sqrt(square_hat) + ADAM_EPS) + decay * param)
    return (moment, square, updated)

def reference(inputs, cotangent, seq_lens, gains, w_qkv, w_out, w_in, w_down, moment_gains, square_gains, moment_qkv, square_qkv, moment_out, square_out, moment_in, square_in, moment_down, square_down):
    params = (gains, w_qkv, w_out, w_in, w_down)

    def group_step(totals, group):
        group_inputs, group_cotangent, lengths = group
        segment, position, valid = layout(lengths, GROUP_TOK)

        def forward(residual, gain_part, qkv_part, out_part, in_part, down_part):
            return forward_group(residual, gain_part, qkv_part, out_part, in_part, down_part, segment, position)
        results, pullback = jax.vjp(forward, group_inputs.astype(jnp.float32), gains, w_qkv, w_out, w_in, w_down)
        grads = pullback(group_cotangent.astype(jnp.float32) * valid.astype(jnp.float32)[:, None])
        totals = tuple((running + grad for running, grad in zip(totals, grads[1:])))
        return (totals, (results, grads[0]))
    initial = tuple((jnp.zeros_like(param) for param in params))
    stacked = (inputs.reshape(GROUPS, GROUP_TOK, D), cotangent.reshape(GROUPS, GROUP_TOK, D), seq_lens)
    totals, (results, grad_rows) = lax.scan(group_step, initial, stacked)
    grad_gains, grad_qkv, grad_out, grad_in, grad_down = totals
    gains_new = adam_step(gains, grad_gains, moment_gains, square_gains, GAIN_RATE, 0.0)
    qkv_new = adam_step(w_qkv, grad_qkv, moment_qkv, square_qkv, LEARN_RATE, WEIGHT_DECAY)
    out_new = adam_step(w_out, grad_out, moment_out, square_out, LEARN_RATE, WEIGHT_DECAY)
    in_new = adam_step(w_in, grad_in, moment_in, square_in, LEARN_RATE, WEIGHT_DECAY)
    down_new = adam_step(w_down, grad_down, moment_down, square_down, LEARN_RATE, WEIGHT_DECAY)
    return (results.reshape(TOKENS, D), grad_rows.reshape(TOKENS, D), gains_new[0], gains_new[1], gains_new[2], qkv_new[0], qkv_new[1], qkv_new[2], out_new[0], out_new[1], out_new[2], in_new[0], in_new[1], in_new[2], down_new[0], down_new[1], down_new[2])
```

```python
import jax
import jax.numpy as jnp
from jax import lax
from jax.experimental import pallas as pl
from jax.experimental.pallas import tpu as pltpu
from jax.sharding import PartitionSpec as P

MAXLEN = 512
QBLOCK = 512
STEP = 10
HEAD_DIM = 64


NORM_EPS = 1e-05
ROPE_BASE = 160000.0
NEG_LARGE = -1000000000.0
BETA_ONE = 0.9
BETA_TWO = 0.98
ADAM_EPS = 1e-06
LEARN_RATE = 0.05
GAIN_RATE = 0.2
WEIGHT_DECAY = 0.01


def layout(lengths, count):
    ends = jnp.cumsum(lengths)
    starts = ends - lengths
    row_ids = jnp.arange(count, dtype=jnp.int32)
    member = (row_ids[:, None] >= starts[None, :]) & (row_ids[:, None] < ends[None, :])
    slot_ids = jnp.arange(lengths.shape[0], dtype=jnp.int32)
    valid = jnp.any(member, axis=1)
    segment = jnp.where(valid, jnp.sum(jnp.where(member, slot_ids[None, :], 0), axis=1), -1)
    position = row_ids - jnp.sum(jnp.where(member, starts[None, :], 0), axis=1)
    return (segment, position, valid)


def rotary(values, position):
    head_size = values.shape[-1]
    half_size = head_size // 2
    exponents = jnp.arange(half_size, dtype=jnp.float32) * (2.0 / head_size)
    frequency = ROPE_BASE ** (-exponents)
    angles = position.astype(jnp.float32)[:, None] * frequency[None, :]
    cosine_table = jnp.concatenate([jnp.cos(angles), jnp.cos(angles)], axis=-1)[:, None, :]
    sine_table = jnp.concatenate([jnp.sin(angles), jnp.sin(angles)], axis=-1)[:, None, :]
    rotated = jnp.concatenate([-values[..., half_size:], values[..., :half_size]], axis=-1)
    return values * cosine_table + rotated * sine_table


def normalize(values):
    centered = values - jnp.mean(values, axis=-1, keepdims=True)
    inverse = lax.rsqrt(jnp.mean(centered * centered, axis=-1, keepdims=True) + NORM_EPS)
    return (centered * inverse, inverse)


def norm_back(grad_normed, normed, inverse):
    first_mean = jnp.mean(grad_normed, axis=-1, keepdims=True)
    second_mean = jnp.mean(grad_normed * normed, axis=-1, keepdims=True)
    return inverse * (grad_normed - first_mean - normed * second_mean)


TILE = 256
PAIR = 2 * HEAD_DIM


def matmul_t(left, right):
    return lax.dot_general(left, right, (((1,), (1,)), ((), ())), preferred_element_type=jnp.float32)


def matmul_n(left, right):
    return lax.dot_general(left, right, (((1,), (0,)), ((), ())), preferred_element_type=jnp.float32)


def matmul_tn(left, right):
    return lax.dot_general(left, right, (((0,), (0,)), ((), ())), preferred_element_type=jnp.float32)


def head_lanes(rows):
    return lax.broadcasted_iota(jnp.int32, (rows, PAIR), 1) // HEAD_DIM


def forward_kernel(seg_q, seg_k, queries, keys, values, mixed, log_totals):
    key_block = keys[...]
    value_block = values[...]
    lanes = head_lanes(TILE)
    for tile in range(queries.shape[0] // TILE):
        rows = pl.ds(tile * TILE, TILE)
        seen = seg_q[rows, :] == seg_k[...]
        query_pair = queries[rows, :]
        parts = []
        for head in range(2):
            query = jnp.where(lanes == head, query_pair, jnp.zeros_like(query_pair))
            scores = jnp.where(seen, matmul_t(query, key_block), NEG_LARGE)
            top = jnp.max(scores, axis=-1, keepdims=True)
            raw = jnp.exp(scores - top)
            total = jnp.sum(raw, axis=-1, keepdims=True)
            weights = (raw * (1.0 / total)).astype(jnp.bfloat16)
            parts.append(matmul_n(weights, value_block))
            log_totals[head, rows, :] = top + jnp.log(total)
        mixed[rows, :] = jnp.where(lanes == 0, parts[0], parts[1]).astype(jnp.bfloat16)


def backward_kernel(seg_q, seg_k, queries, keys, values, grad_mixed, log_totals, grad_q, grad_k, grad_v):
    key_block = keys[...]
    value_block = values[...]
    lanes = head_lanes(TILE)
    for tile in range(queries.shape[0] // TILE):
        rows = pl.ds(tile * TILE, TILE)
        seen = seg_q[rows, :] == seg_k[...]
        query_pair = queries[rows, :]
        grad_pair = grad_mixed[rows, :]
        parts = []
        for head in range(2):
            query = jnp.where(lanes == head, query_pair, jnp.zeros_like(query_pair))
            grad = jnp.where(lanes == head, grad_pair, jnp.zeros_like(grad_pair))
            scores = jnp.where(seen, matmul_t(query, key_block), NEG_LARGE)
            probs = jnp.exp(scores - log_totals[head, rows, :])
            grad_probs = matmul_t(grad, value_block)
            inner = jnp.sum(probs * grad_probs, axis=-1, keepdims=True)
            grad_scores = (probs * (grad_probs - inner)).astype(jnp.bfloat16)
            parts.append(matmul_n(grad_scores, key_block))
            key_part = matmul_tn(grad_scores, query)
            value_part = matmul_tn(probs.astype(jnp.bfloat16), grad)
            if tile == 0 and head == 0:
                grad_k[...] = key_part
                grad_v[...] = value_part
            else:
                grad_k[...] += key_part
                grad_v[...] += value_part
        grad_q[rows, :] = jnp.where(lanes == 0, parts[0], parts[1]) * (HEAD_DIM**-0.5)


def attention_specs(rows, window):
    whole_q = pl.BlockSpec((rows, 1), lambda pair: (0, 0))
    whole_k = pl.BlockSpec((1, window), lambda pair: (0, 0))
    by_rows = pl.BlockSpec((rows, PAIR), lambda pair: (0, pair))
    by_window = pl.BlockSpec((window, PAIR), lambda pair: (0, pair))
    totals = pl.BlockSpec((2, rows, 1), lambda pair: (pair, 0, 0))
    return whole_q, whole_k, by_rows, by_window, totals


def attend_forward(seg_q, seg_k, queries, keys, values):
    rows, width = queries.shape
    window = keys.shape[0]
    whole_q, whole_k, by_rows, by_window, totals = attention_specs(rows, window)
    return pl.pallas_call(
        forward_kernel,
        grid=(width // PAIR,),
        in_specs=[whole_q, whole_k, by_rows, by_window, by_window],
        out_specs=[by_rows, totals],
        out_shape=[
            jax.ShapeDtypeStruct((rows, width), jnp.bfloat16),
            jax.ShapeDtypeStruct((width // HEAD_DIM, rows, 1), jnp.float32),
        ],
        compiler_params=pltpu.CompilerParams(vmem_limit_bytes=48 * 1024 * 1024),
        cost_estimate=pl.CostEstimate(
            flops=4 * rows * window * width, bytes_accessed=8 * window * width, transcendentals=rows * window * 16
        ),
        name="attend_forward",
    )(seg_q, seg_k, queries, keys, values)


def attend_backward(seg_q, seg_k, queries, keys, values, grad_mixed, log_totals):
    rows, width = queries.shape
    window = keys.shape[0]
    whole_q, whole_k, by_rows, by_window, totals = attention_specs(rows, window)
    return pl.pallas_call(
        backward_kernel,
        grid=(width // PAIR,),
        in_specs=[whole_q, whole_k, by_rows, by_window, by_window, by_rows, totals],
        out_specs=[by_rows, by_window, by_window],
        out_shape=[
            jax.ShapeDtypeStruct((rows, width), jnp.float32),
            jax.ShapeDtypeStruct((window, width), jnp.float32),
            jax.ShapeDtypeStruct((window, width), jnp.float32),
        ],
        compiler_params=pltpu.CompilerParams(vmem_limit_bytes=48 * 1024 * 1024),
        cost_estimate=pl.CostEstimate(
            flops=10 * rows * window * width, bytes_accessed=16 * window * width, transcendentals=rows * window * 16
        ),
        name="attend_backward",
    )(seg_q, seg_k, queries, keys, values, grad_mixed, log_totals)


def halve(blocks, axis, name, bit):
    mine = (lax.axis_index(name) >> bit) & 1
    keep = lax.dynamic_index_in_dim(blocks, mine, axis, keepdims=False)
    send = lax.dynamic_index_in_dim(blocks, 1 - mine, axis, keepdims=False)
    pairs = [(i, i ^ (1 << bit)) for i in range(lax.axis_size(name))]
    return keep.astype(jnp.float32) + lax.ppermute(send, name, pairs).astype(jnp.float32)


def dp_halves(grads, axis, turned):
    bits = (lax.axis_size("dp") - 1).bit_length()
    shape = grads.shape
    blocks = grads.reshape(*shape[:axis], *[2] * bits, shape[axis] >> bits, *shape[axis + 1 :])
    left = list(range(bits - 1, -1, -1))
    order = [0] + (list(range(bits - 1, 0, -1)) if turned else list(range(1, bits)))
    for bit in order:
        place = left.index(bit)
        blocks = halve(blocks, axis + place, "dp", bit).astype(jnp.bfloat16)
        left.pop(place)
    return blocks


def tensor_halves(blocks):
    bits = (lax.axis_size("tensor") - 1).bit_length()
    blocks = blocks.reshape(*[2] * bits, *blocks.shape[1:])
    for bit in range(bits):
        blocks = halve(blocks.astype(jnp.bfloat16), bits - 1 - bit, "tensor", bit)
    return blocks


def adam_step(param, grad, moment, square, rate, decay):
    moment = BETA_ONE * moment + (1.0 - BETA_ONE) * grad
    square = BETA_TWO * square + (1.0 - BETA_TWO) * grad * grad
    moment_hat = moment / (1.0 - BETA_ONE**STEP)
    square_hat = square / (1.0 - BETA_TWO**STEP)
    updated = param - rate * (moment_hat / (jnp.sqrt(square_hat) + ADAM_EPS) + decay * param)
    return (moment, square, updated)


def gated(pre_part, gate_part):
    return jax.nn.gelu(pre_part, approximate=False) * gate_part


def body(
    inputs,
    cotangent,
    seq_lens,
    gains,
    w_qkv,
    w_out,
    w_in,
    w_down,
    moment_gains,
    square_gains,
    moment_qkv,
    square_qkv,
    moment_out,
    square_out,
    moment_in,
    square_in,
    moment_down,
    square_down,
):
    both = ("dp", "tensor")
    dp_size, tp_size = lax.axis_size("dp"), lax.axis_size("tensor")
    local_rows, width = inputs.shape
    heads = width // HEAD_DIM
    group_rows = local_rows * tp_size
    my_index = lax.axis_index("tensor")
    my_start = my_index * local_rows
    half = jnp.bfloat16
    upward = [(i, i + 1) for i in range(tp_size - 1)]
    downward = [(i + 1, i) for i in range(tp_size - 1)]

    depth, qkv_cols = w_qkv.shape[1], w_qkv.shape[2]
    first_rows_count = 4 * depth
    gain_cols = gains.shape[1]
    gain_row = jnp.pad(gains.astype(half).reshape(1, 2 * gain_cols), ((0, 15), (0, qkv_cols - 2 * gain_cols)))
    first_pack = jnp.concatenate(
        [w_qkv.astype(half).reshape(3 * depth, qkv_cols), w_out.astype(half).T, gain_row]
    )
    units = w_in.shape[2]
    second_pack = jnp.concatenate([w_in.astype(half).transpose(0, 2, 1), w_down.astype(half)[None]])
    first_all = lax.all_gather(first_pack, both, axis=0)
    second_all = lax.all_gather(second_pack, both, axis=0)

    first_all = first_all.reshape(dp_size, tp_size, first_rows_count + 16, qkv_cols)
    gain_values = (
        first_all[:, 0, first_rows_count, : 2 * gain_cols]
        .reshape(dp_size, 2, gain_cols).transpose(1, 0, 2).reshape(2, width)
    ).astype(jnp.float32)
    first_full = (
        first_all[:, :, :first_rows_count].reshape(dp_size, tp_size, 4, depth, qkv_cols)
        .transpose(2, 0, 3, 1, 4).reshape(4, width, width)
    )
    qkv_full, out_full = first_full[:3], first_full[3]
    second_full = (
        second_all.reshape(dp_size, tp_size, 3, units, depth).transpose(1, 2, 3, 0, 4)
        .reshape(tp_size, 3, units, width)
    )
    in_full, down_full = second_full[:, :2], second_full[:, 2]

    segment, position, valid = layout(seq_lens[0], group_rows)
    my_valid = lax.dynamic_slice_in_dim(valid, my_start, local_rows, 0).astype(jnp.float32)
    segment = jnp.where(valid, segment, -2 - jnp.arange(group_rows, dtype=jnp.int32))
    pad_segment = jnp.pad(segment, (MAXLEN, MAXLEN), constant_values=-1)
    pad_position = jnp.pad(position, (MAXLEN, MAXLEN))
    window = local_rows + 2 * MAXLEN
    seg_k = lax.dynamic_slice_in_dim(pad_segment, my_start, window, 0)
    pos_k = lax.dynamic_slice_in_dim(pad_position, my_start, window, 0)
    seg_q = seg_k[MAXLEN : MAXLEN + local_rows]
    mine = slice(MAXLEN, MAXLEN + local_rows)

    before = lax.ppermute(inputs[local_rows - MAXLEN :], "tensor", upward)
    after = lax.ppermute(inputs[:MAXLEN], "tensor", downward)
    wide = jnp.concatenate([before, inputs, after]).astype(jnp.float32)
    residual = inputs.astype(jnp.float32)
    normed_wide, inverse_wide = normalize(wide)
    first_rows = (normed_wide * gain_values[0]).astype(half)
    normed_one, inverse_one = normed_wide[mine], inverse_wide[mine]

    def project(rows, weight):
        return jnp.dot(rows, weight, preferred_element_type=jnp.float32)

    def turn(values):
        return rotary(values.reshape(window, heads, HEAD_DIM), pos_k).reshape(window, width)

    def turn_own(values):
        return rotary(values.reshape(local_rows, heads, HEAD_DIM), pos_k[mine]).reshape(local_rows, width)

    query_raw = project(first_rows[mine], qkv_full[0])
    key_raw = project(first_rows, qkv_full[1])
    queries = turn_own(query_raw).astype(half) * half(HEAD_DIM**-0.5)
    keys = turn(key_raw).astype(half)
    values = project(first_rows, qkv_full[2]).astype(half)
    seg_q, seg_k = seg_q[:, None], seg_k[None, :]
    attended, log_totals = attend_forward(seg_q, seg_k, queries, keys, values)
    middle = residual + jnp.einsum("rc,dc->rd", attended, out_full, preferred_element_type=jnp.float32)
    normed_two, inverse_two = normalize(middle)
    second_rows = (normed_two * gain_values[1]).astype(half)
    expanded = jnp.einsum("rd,tkfd->tkrf", second_rows, in_full, preferred_element_type=jnp.float32)
    hidden_full, gated_back = jax.vjp(gated, expanded[:, 0], expanded[:, 1])
    hidden = hidden_full.astype(half)
    outputs = middle + jnp.einsum("trf,tfd->rd", hidden, down_full, preferred_element_type=jnp.float32)

    grad_masked = cotangent.astype(jnp.float32) * my_valid[:, None]
    grad_rows = grad_masked.astype(half)

    def second_share(grads, turn_y):
        blocks = dp_halves(grads.astype(half), 1, turn_y)
        return tensor_halves(blocks)

    grad_down = jnp.einsum("rd,trf->tdf", grad_rows, hidden, preferred_element_type=jnp.float32)
    down_sum = second_share(grad_down, False).T
    grad_hidden = jnp.einsum("rd,tfd->trf", grad_rows, down_full, preferred_element_type=jnp.float32)
    grad_pre, grad_gate = gated_back(grad_hidden)
    grad_expanded = jnp.stack([grad_pre, grad_gate], axis=1).astype(half)
    grad_in_first = jnp.einsum("rd,trf->tdf", second_rows, grad_pre.astype(half), preferred_element_type=jnp.float32)
    grad_in_second = jnp.einsum("rd,trf->tdf", second_rows, grad_gate.astype(half), preferred_element_type=jnp.float32)
    in_sum = jnp.stack([second_share(grad_in_first, True), second_share(grad_in_second, False)])
    grad_second = jnp.einsum("tkrf,tkfd->rd", grad_expanded, in_full, preferred_element_type=jnp.float32)
    gain_two = jnp.sum(grad_second * normed_two, axis=0)
    grad_middle = grad_masked + norm_back(grad_second * gain_values[1], normed_two, inverse_two)
    middle_rows = grad_middle.astype(half)
    grad_out = jnp.einsum("rd,rc->dc", middle_rows, attended, preferred_element_type=jnp.float32).astype(half)
    grad_attended = jnp.einsum("rd,dc->rc", middle_rows, out_full, preferred_element_type=jnp.float32).astype(half)
    grad_q, grad_k, grad_v = attend_backward(seg_q, seg_k, queries, keys, values, grad_attended, log_totals)
    unused, turn_back = jax.vjp(turn, key_raw)
    unused, turn_own_back = jax.vjp(turn_own, query_raw)
    grad_q = turn_own_back(grad_q)[0].astype(half)
    grad_k = turn_back(grad_k)[0].astype(half)
    grad_v = grad_v.astype(half)

    def back(grads, weight):
        return jnp.einsum("rc,dc->rd", grads, weight, preferred_element_type=jnp.float32)

    grad_wide = back(grad_k, qkv_full[1]) + back(grad_v, qkv_full[2])
    grad_own = grad_wide[mine] + back(grad_q, qkv_full[0])
    from_above = lax.ppermute(grad_wide[:MAXLEN].astype(half), "tensor", downward)
    from_below = lax.ppermute(grad_wide[MAXLEN + local_rows :].astype(half), "tensor", upward)
    gain_one = (
        jnp.sum(grad_own * normed_one, axis=0)
        + jnp.sum(grad_wide[:MAXLEN] * normed_wide[:MAXLEN], axis=0)
        + jnp.sum(grad_wide[MAXLEN + local_rows :] * normed_wide[MAXLEN + local_rows :], axis=0)
    )

    def outer(rows, grads):
        return jnp.einsum("rd,rc->dc", rows, grads, preferred_element_type=jnp.float32).astype(half)

    gain_blocks = jnp.stack([gain_one, gain_two]).reshape(2, dp_size, gain_cols).transpose(1, 0, 2)
    gain_blocks = jnp.pad(
        gain_blocks.astype(half).reshape(dp_size, 1, 1, 2 * gain_cols),
        ((0, 0), (0, 15), (0, 0), (0, qkv_cols - 2 * gain_cols)),
    )
    gain_blocks = jnp.broadcast_to(gain_blocks, (dp_size, 16, tp_size, qkv_cols)).reshape(dp_size, 16, width)

    def rows_of(grads):
        return grads.reshape(dp_size, depth, width)

    def first_share(parts, turn_y):
        packed = jnp.concatenate(parts, axis=1)
        count = packed.shape[1]
        block = dp_halves(packed.reshape(dp_size * count, width), 0, turn_y)
        return tensor_halves(block.reshape(count, tp_size, qkv_cols).transpose(1, 0, 2))

    value_out = first_share(
        [rows_of(outer(first_rows, grad_v)), rows_of(grad_out)], False
    )
    query_key = first_share(
        [rows_of(outer(first_rows[mine], grad_q)), rows_of(outer(first_rows, grad_k)), gain_blocks], True
    )
    qkv_sum = jnp.concatenate([query_key[: 2 * depth], value_out[:depth]]).reshape(w_qkv.shape)
    out_sum = value_out[depth:].T
    gain_grads = query_key[2 * depth, : 2 * gain_cols].reshape(2, gain_cols)

    shift_low = jnp.pad(from_below.astype(jnp.float32), ((0, local_rows - MAXLEN), (0, 0)))
    shift_high = jnp.pad(from_above.astype(jnp.float32), ((local_rows - MAXLEN, 0), (0, 0)))
    grad_first = grad_own + shift_low + shift_high
    grad_inputs = grad_middle + norm_back(grad_first * gain_values[0], normed_one, inverse_one)
    gains_new = adam_step(gains, gain_grads, moment_gains, square_gains, GAIN_RATE, 0.0)
    qkv_new = adam_step(w_qkv, qkv_sum, moment_qkv, square_qkv, LEARN_RATE, WEIGHT_DECAY)
    out_new = adam_step(w_out, out_sum, moment_out, square_out, LEARN_RATE, WEIGHT_DECAY)
    in_new = adam_step(w_in, in_sum, moment_in, square_in, LEARN_RATE, WEIGHT_DECAY)
    down_new = adam_step(w_down, down_sum, moment_down, square_down, LEARN_RATE, WEIGHT_DECAY)
    return (
        outputs,
        grad_inputs,
        gains_new[0],
        gains_new[1],
        gains_new[2],
        qkv_new[0],
        qkv_new[1],
        qkv_new[2],
        out_new[0],
        out_new[1],
        out_new[2],
        in_new[0],
        in_new[1],
        in_new[2],
        down_new[0],
        down_new[1],
        down_new[2],
    )


def solution(mesh):
    in_specs = (
        P(("dp", "tensor"), None),
        P(("dp", "tensor"), None),
        P("dp", None),
        P(None, "dp"),
        P(None, "dp", "tensor"),
        P("tensor", "dp"),
        P(None, "dp", "tensor"),
        P("tensor", "dp"),
        P(None, "dp"),
        P(None, "dp"),
        P(None, "dp", "tensor"),
        P(None, "dp", "tensor"),
        P("tensor", "dp"),
        P("tensor", "dp"),
        P(None, "dp", "tensor"),
        P(None, "dp", "tensor"),
        P("tensor", "dp"),
        P("tensor", "dp"),
    )
    out_specs = (
        P(("dp", "tensor"), None),
        P(("dp", "tensor"), None),
        P(None, "dp"),
        P(None, "dp"),
        P(None, "dp"),
        P(None, "dp", "tensor"),
        P(None, "dp", "tensor"),
        P(None, "dp", "tensor"),
        P("tensor", "dp"),
        P("tensor", "dp"),
        P("tensor", "dp"),
        P(None, "dp", "tensor"),
        P(None, "dp", "tensor"),
        P(None, "dp", "tensor"),
        P("tensor", "dp"),
        P("tensor", "dp"),
        P("tensor", "dp"),
    )
    return jax.shard_map(body, mesh=mesh, in_specs=in_specs, out_specs=out_specs, check_vma=False)
```
